32 devices in a mesh: dp: 8 (over z, x), seq: 4 (over y, core).
Axes of the slice: x: 2, y: 2, z: 4, core: 2. Of those that a mesh axis runs over, the one named last changes fastest.
Arguments:
- hidden_in: bfloat16 [8, 1024, 2048], P('dp', 'seq'), may hold values from -6 to 6
- doc_lengths: int32 [8, 4], P('dp'), may hold values from 1 to 512, 1024 in all within a row
- norm1_gain: bfloat16 [2048], P(('dp', 'seq')), may hold values from 0.5 to 1.5
- w_qkv: bfloat16 [2048, 6144], P(('dp', 'seq')), may hold values from -0.125 to 0.125
- conv_weight: bfloat16 [4, 6144], P(None, ('dp', 'seq')), may hold values from -3 to 3
- w_beta: bfloat16 [2048, 16], P(('dp', 'seq')), may hold values from -0.125 to 0.125
- head_gain: bfloat16 [2048], P(('dp', 'seq')), may hold values from 0.5 to 1.5
- w_out: bfloat16 [2048, 2048], P(('dp', 'seq')), may hold values from -0.125 to 0.125
- norm2_gain: bfloat16 [2048], P(('dp', 'seq')), may hold values from 0.5 to 1.5
- w_gate_up: bfloat16 [2048, 2, 5632], P('dp', None, 'seq'), may hold values from -0.125 to 0.125
- w_down: bfloat16 [5632, 2048], P('seq', 'dp'), may hold values from -0.15625 to 0.15625
- cotangent: bfloat16 [8, 1024, 2048], P('dp', 'seq'), may hold values from -6 to 6
Outputs:
- out: bfloat16 [8, 1024, 2048], P('dp', 'seq')
- grad_x: float32 [8, 1024, 2048], P('dp', 'seq')
- grad_norm1_gain: float32 [2048], P(('dp', 'seq'))
- grad_w_qkv: float32 [2048, 6144], P(('dp', 'seq'))
- grad_conv_weight: float32 [4, 6144], P(None, ('dp', 'seq'))
- grad_w_beta: float32 [2048, 16], P(('dp', 'seq'))
- grad_head_gain: float32 [2048], P(('dp', 'seq'))
- grad_w_out: float32 [2048, 2048], P(('dp', 'seq'))
- grad_norm2_gain: float32 [2048], P(('dp', 'seq'))
- grad_w_gate_up: float32 [2048, 2, 5632], P('dp', None, 'seq')
- grad_w_down: float32 [5632, 2048], P('seq', 'dp')
The draws below stay inside these ranges and needn't reach their ends.
Inputs may be any that keep to these rules, and one draw needn't show every extreme that they name: `doc_lengths`: each row's 4 lengths sum to 1024; in every row the longest is 512.
All inputs are finite; a program needn't handle non-finite values.
Results may differ from the reference program's by a relative error of at most 0.017.
Values may be sent and summed in bfloat16 or wider, within the bound.
No kernel may reach another device: no remote copies, remote signals or barrier semaphores. Data moves between devices by JAX's collectives and lax.ppermute only.
A program may use at most 448 MiB of HBM per device.

```python
import math
import jax
import jax.numpy as jnp
import numpy as np
from jax import lax

D = 2048
H = 16
HD = 128
FF = 5632
KCONV = 4
SPAN = 64
NDOC = 4
SEQ_LEN = 1024
ROWS = 8


def shard_levels(stream_key, extent, split, low, largest):
    loudness = 1.0
    for position, blocks in split:
        steps = jax.random.uniform(jax.random.fold_in(jax.random.fold_in(stream_key, 6), position), (blocks,), jnp.float32, low / len(split), largest / len(split))
        loudness = loudness * jnp.repeat(jnp.exp(steps), extent[position] // blocks).reshape((-1,) + (1,) * (len(extent) - 1 - position))
    return loudness


def length_profile(count, total, most, slope):
    loads = [(1 << 20) // math.isqrt(grade ** slope) + 1 for grade in range(2, count + 1)]
    rest, holding = total - most - (count - 1), [1] * (count - 1)
    while rest > 0:
        free = [i for i in range(count - 1) if holding[i] < most]
        mass, left = sum([loads[i] for i in free]), rest
        for i in free:
            more = min(most - holding[i], max(1, left * loads[i] // mass), rest)
            holding[i] = holding[i] + more
            rest = rest - more
    return np.array([most] + holding)


def ragged(own_key, amount, total, most, lean):
    if amount == 2:
        one = jax.random.randint(own_key, (), max(1, total - most), min(most, total - 1) + 1)
        return jnp.stack([one, total - one])
    lengths = jnp.asarray(length_profile(amount, total, most, lean), jnp.int32)
    twos = (amount - 1) // 2
    giver, sink = lengths[1:1 + 2 * twos:2], lengths[2:2 + 2 * twos:2]
    margin = jnp.minimum(giver - 1, most - sink)
    passed = jax.random.randint(jax.random.fold_in(own_key, 1), (twos,), 0, 1 << 20) % (margin + 1)
    lengths = lengths.at[1:1 + 2 * twos:2].set(giver - passed).at[2:2 + 2 * twos:2].set(sink + passed)
    return lengths[jax.random.permutation(jax.random.fold_in(own_key, 2), amount)]


def gaussian(stream_key, dims, scale, reach, shards=(), kind=jnp.bfloat16):
    loudness = shard_levels(stream_key, dims, shards, -0.22, 0.18) if shards else 1.0
    entries = jax.random.normal(stream_key, dims, jnp.float32) * scale * loudness
    return jnp.minimum(jnp.maximum(entries, -reach), reach).astype(kind)


def setup_inputs(seed: int = 0) -> dict:
    key_list = jax.random.split(jax.random.key(seed), 13)
    return {
        "hidden_in": gaussian(key_list[0], (ROWS, SEQ_LEN, D), 1.0, 6.0, ((0, 8), (1, 4))),
        "doc_lengths": jax.vmap(lambda own: ragged(own, NDOC, SEQ_LEN, SEQ_LEN // 2, 1))(jax.random.split(key_list[1], ROWS)).reshape((ROWS, NDOC)).astype(jnp.int32),
        "norm1_gain": jnp.clip(1.0 + 0.1 * jax.random.normal(key_list[2], (D,), jnp.float32), 0.5, 1.5).astype(jnp.bfloat16),
        "w_qkv": gaussian(key_list[3], (D, 3 * D), D ** -0.5, 0.125, ((0, 32),)),
        "conv_weight": gaussian(key_list[4], (KCONV, 3 * D), 0.5, 3.0, ((1, 32),)),
        "w_beta": gaussian(key_list[5], (D, H), D ** -0.5, 0.125, ((0, 32),)),
        "head_gain": jnp.clip(1.0 + 0.1 * jax.random.normal(key_list[6], (D,), jnp.float32), 0.5, 1.5).astype(jnp.bfloat16),
        "w_out": gaussian(key_list[7], (D, D), D ** -0.5, 0.125, ((0, 32),)),
        "norm2_gain": jnp.clip(1.0 + 0.1 * jax.random.normal(key_list[8], (D,), jnp.float32), 0.5, 1.5).astype(jnp.bfloat16),
        "w_gate_up": gaussian(key_list[9], (D, 2, FF), D ** -0.5, 0.125, ((0, 8), (2, 4))),
        "w_down": gaussian(key_list[10], (FF, D), (FF // 4) ** -0.5, 0.15625, ((0, 4), (1, 8))),
        "cotangent": gaussian(key_list[11], (ROWS, SEQ_LEN, D), 1.0, 6.0, ((0, 8), (1, 4))),
    }


@jax.custom_vjp
def low(v):
    return lax.optimization_barrier(v.astype(jnp.bfloat16)).astype(jnp.float32)

@jax.custom_vjp
def low_back(v):
    return v

def low_keep(v):
    return (low(v), None)

def low_pass(kept, grad):
    return (grad,)

def back_keep(v):
    return (v, None)

def back_low(kept, grad):
    return (low(grad),)
low.defvjp(low_keep, low_pass)
low_back.defvjp(back_keep, back_low)
HIGH = lax.Precision.HIGHEST
EPS = 1e-05
UNIT_EPS = 1e-06

def low_both(values):
    return low_back(low(values))

def rms_norm(values, gain):
    return values * lax.rsqrt(lax.optimization_barrier(jnp.mean(values * values, axis=-1, keepdims=True)) + EPS) * gain

def unit_heads(values):
    shaped = values.reshape(values.shape[:-1] + (H, HD))
    return shaped * lax.rsqrt(lax.optimization_barrier(jnp.sum(shaped * shaped, axis=-1, keepdims=True)) + UNIT_EPS)

def delta_token(memory, inputs):
    query_now, key_now, value_now, rate_now, fresh_now = inputs
    memory = memory * (1.0 - fresh_now)[:, None, None, None]
    predicted = jnp.einsum('ghij,ghj->ghi', memory, key_now, precision=HIGH)
    update = rate_now[..., None] * (value_now - predicted)
    memory = memory + update[..., :, None] * key_now[..., None, :]
    output = jnp.einsum('ghij,ghj->ghi', memory, query_now, precision=HIGH)
    return (memory, output)

@jax.checkpoint
def delta_block(memory, block_in):
    return lax.scan(delta_token, memory, block_in)

def delta_rule(queries, key_rows, value_rows, rates, fresh):
    per_group = queries.shape[0]

    def to_time(array):
        moved = jnp.moveaxis(array, 1, 0)
        return moved.reshape((SEQ_LEN // SPAN, SPAN) + moved.shape[1:])
    memory = jnp.zeros((per_group, H, HD, HD), jnp.float32)
    _, outputs = lax.scan(delta_block, memory, (to_time(queries), to_time(key_rows), to_time(value_rows), to_time(rates), to_time(fresh)))
    return jnp.moveaxis(outputs.reshape((SEQ_LEN,) + outputs.shape[2:]), 0, 1)

def reference(hidden_in, doc_lengths, norm1_gain, w_qkv, conv_weight, w_beta, head_gain, w_out, norm2_gain, w_gate_up, w_down, cotangent):
    doc_ends = jnp.cumsum(doc_lengths, axis=1)
    starts = doc_ends - doc_lengths
    places = jnp.arange(SEQ_LEN, dtype=jnp.int32)
    starts_at = lax.optimization_barrier(jnp.max(jnp.where(starts[:, None, :] <= places[None, :, None], starts[:, None, :], 0), axis=2)).astype(jnp.int32)
    per_group = math.gcd(ROWS, max(1, 4096 // SEQ_LEN))
    groups = ROWS // per_group

    @jax.checkpoint
    def group_forward(weights, rows_in, table):
        gain_one, mat_qkv, conv_taps, mat_beta, gain_head, mat_out, gain_two, mat_gu, mat_down = weights
        normed = low(rms_norm(rows_in, gain_one))
        linear = low_both(jnp.einsum('gtd,de->gte', normed, mat_qkv, precision=HIGH))
        beta_lin = low_back(jnp.einsum('gtd,dh->gth', normed, mat_beta, precision=HIGH))
        convolved = jnp.zeros_like(linear)
        for delay in range(KCONV):
            shifted = jnp.pad(linear, ((0, 0), (delay, 0), (0, 0)))[:, :SEQ_LEN]
            inside = (places[None, :] - delay >= table).astype(jnp.float32)[..., None]
            convolved = convolved + conv_taps[delay] * shifted * inside
        acts = jax.nn.silu(convolved)
        queries = unit_heads(acts[..., :D])
        key_rows = unit_heads(acts[..., D:2 * D])
        value_rows = acts[..., 2 * D:].reshape(acts.shape[:2] + (H, HD))
        rates = jax.nn.sigmoid(beta_lin)
        fresh = (places[None, :] == table).astype(jnp.float32)
        mixed = delta_rule(queries, key_rows, value_rows, rates, fresh)
        head_stat = lax.rsqrt(lax.optimization_barrier(jnp.mean(mixed * mixed, axis=-1, keepdims=True)) + EPS)
        head_low = low((mixed * head_stat * gain_head.reshape(H, HD)).reshape(mixed.shape[:2] + (D,)))
        attn = low_back(jnp.einsum('gtd,de->gte', head_low, mat_out, precision=HIGH))
        middle = rows_in + attn
        normed_two = low(rms_norm(middle, gain_two))
        gate_up = low_back(jnp.einsum('gtd,dk->gtk', normed_two, mat_gu.reshape(D, 2 * FF), precision=HIGH))
        act_low = low(jax.nn.silu(gate_up[..., :FF]) * gate_up[..., FF:])
        return middle + jnp.einsum('gtf,fd->gtd', act_low, mat_down, precision=HIGH)

    def all_forward(inputs, weights):
        shaped = inputs.reshape(groups, per_group, SEQ_LEN, D)
        tables = starts_at.reshape(groups, per_group, SEQ_LEN)

        def advance(carried, element):
            return (carried, group_forward(weights, element[0], element[1]))
        _, results = lax.scan(advance, jnp.zeros((), jnp.float32), (shaped, tables))
        return results.reshape(ROWS, SEQ_LEN, D)
    weights = tuple((item.astype(jnp.float32) for item in (norm1_gain, w_qkv, conv_weight, w_beta, head_gain, w_out, norm2_gain, w_gate_up, w_down)))
    result, pullback = jax.vjp(all_forward, hidden_in.astype(jnp.float32), weights)
    input_grad, weight_grads = pullback(cotangent.astype(jnp.float32))
    return (result.astype(jnp.bfloat16), input_grad, weight_grads[0], weight_grads[1], weight_grads[2], weight_grads[3], weight_grads[4], weight_grads[5], weight_grads[6], weight_grads[7], weight_grads[8])
```

```python
import functools
import jax
import jax.numpy as jnp
from jax import lax
from jax.experimental import pallas as pl
from jax.experimental.pallas import tpu as pltpu
from jax.sharding import Mesh, PartitionSpec as P

KCONV = 4
HD = 128
EPS = 1e-05
UNIT_EPS = 1e-06
F32 = jnp.float32
BF16 = jnp.bfloat16


def mm(left, right, dim_left=1, dim_right=0):
    return lax.dot_general(
        left.astype(BF16),
        right.astype(BF16),
        (((dim_left,), (dim_right,)), ((), ())),
        preferred_element_type=F32,
    )


def split(value):
    high = value.astype(BF16)
    return high, (value - high.astype(F32)).astype(BF16)


def mm3(left, right):
    lh, ll = split(left)
    rh, rl = split(right)
    return mm(lh, rh) + (mm(lh, rl) + mm(ll, rh))


def iota(shape, dim):
    return lax.broadcasted_iota(jnp.int32, shape, dim)


def doc_start(starts, row, place):
    found = jnp.zeros_like(place)
    for j in range(starts.shape[1]):
        first = starts[row, j]
        found = jnp.maximum(found, jnp.where(first <= place, first, 0))
    return found


def scalar_start(starts, row, place):
    found = jnp.int32(0)
    for j in range(starts.shape[1]):
        first = starts[row, j]
        found = jnp.maximum(found, jnp.where(first <= place, first, 0))
    return found


def shift_down(cur, tail, by):
    if by == 0:
        return cur
    rolled = pltpu.roll(cur, by, 0)
    edge = pltpu.roll(tail, by, 0)
    top = jnp.where(iota(edge.shape, 0) < by, edge, rolled[:8])
    return jnp.concatenate([top, rolled[8:]], axis=0)


def shift_up(cur, head, by):
    if by == 0:
        return cur
    size = cur.shape[0]
    rolled = pltpu.roll(cur, size - by, 0)
    edge = pltpu.roll(head, 8 - by, 0)
    last = jnp.where(iota(edge.shape, 0) >= 8 - by, edge, rolled[size - 8 :])
    return jnp.concatenate([rolled[: size - 8], last], axis=0)


class Masks:
    def __init__(self, starts, row, base, size):
        place = base + iota((size, HD), 0)
        start = doc_start(starts, row, place)
        self.inside = [(place - i >= start).astype(F32) for i in range(KCONV)]
        self.carry_in = (start < base).astype(F32)
        last = scalar_start(starts, row, base + size - 1)
        self.last_doc = (start == last).astype(F32)
        self.carry_last = (last < base).astype(F32)
        rows, cols = iota((size, size), 0), iota((size, size), 1)
        start_row = doc_start(starts, row, base + rows)
        start_col = doc_start(starts, row, base + cols)
        same = start_row == start_col
        self.strict = (same & (rows > cols)).astype(F32)
        self.diag = (same & (rows >= cols)).astype(F32)
        self.diag_t = (same & (rows <= cols)).astype(F32)


def conv_of(cur, tail, taps, masks):
    shifted = [shift_down(cur, tail, i) * masks.inside[i] for i in range(KCONV)]
    total = shifted[0] * taps[0:1]
    for i in range(1, KCONV):
        total = total + shifted[i] * taps[i : i + 1]
    return shifted, total


def unit(values):
    return lax.rsqrt(jnp.sum(values * values, axis=-1, keepdims=True) + UNIT_EPS)


def inverse(lower, size):
    rows, cols = iota((size, size), 0), iota((size, size), 1)
    low = jnp.where((rows // 16) == (cols // 16), lower, 0.0)
    eye = (rows == cols).astype(F32)
    square = mm3(low, low)
    found = eye - low
    found = found + mm3(found, square)
    square = mm3(square, square)
    found = found + mm3(found, square)
    square = mm3(square, square)
    found = found + mm3(found, square)
    width = 16
    while width < size:
        cross = jnp.where(
            ((rows // (2 * width)) == (cols // (2 * width))) & ((rows // width) != (cols // width)),
            lower,
            0.0,
        )
        found = found - mm3(mm3(found, cross), found)
        width *= 2
    return found


def forward_kernel(heads, rows, size, starts, place, lin, taps, gain, low_out, mixed_out, inv_out, fix_out, err_out, mem_out, memory, tails):
    step = pl.program_id(0)
    base = step * size

    @pl.when(step == 0)
    def _():
        memory[...] = jnp.zeros_like(memory)
        tails[...] = jnp.zeros_like(tails)

    for row in range(rows):
        masks = Masks(starts, row, base, size)
        for head in range(heads):
            pair = row * heads + head

            def group(kind):
                at = (kind * heads + head) * HD
                cur = lin[0, 0, row, 0, :, at : at + HD].astype(BF16).astype(F32)
                tail = tails[row, :, at : at + HD]
                _, conv = conv_of(cur, tail, taps[:, at : at + HD], masks)
                tails[row, :, at : at + HD] = cur[size - 8 :]
                return conv * jax.nn.sigmoid(conv)

            query, key, value = group(0), group(1), group(2)
            query = query * unit(query)
            key = key * unit(key)
            at = 3 * heads * HD + head
            rate = jnp.broadcast_to(
                jax.nn.sigmoid(lin[0, 0, row, 0, :, at : at + 1]), (size, HD)
            )
            rate_sq = rate if size == HD else rate[:, :size]
            stacked = jnp.concatenate([query, key], axis=0)
            gram = mm(stacked, key, 1, 1)
            inv = inverse(rate_sq * gram[size:] * masks.strict, size)
            attend = gram[:size] * masks.diag
            state = memory[pair]
            read = mm(stacked, state)
            error = value - masks.carry_in * read[size:]
            fix = mm(inv, rate * error)
            mixed = masks.carry_in * read[:size] + mm(attend, fix)
            memory[pair] = masks.carry_last * state + mm(key * masks.last_doc, fix, 0, 0)
            stat = lax.rsqrt(jnp.mean(mixed * mixed, axis=-1, keepdims=True) + EPS)
            at = head * HD
            low_out[0, 0, row, 0, :, at : at + HD] = (mixed * stat * gain[:, at : at + HD]).astype(BF16)
            mixed_out[0, 0, row, 0, :, at : at + HD] = mixed
            inv_out[0, pair] = inv.astype(BF16)
            fix_out[0, pair] = fix
            err_out[0, pair] = error
            mem_out[0, pair] = state


def backward_kernel(heads, rows, size, steps, starts, place, lin, edge, taps, gain, mixed_in, grad_in, inv_in, fix_in, err_in, mem_in, dlin_out, dtaps_out, dgain_out, dmemory, nexts):
    step = pl.program_id(0)
    chunk = steps - 1 - step
    base = chunk * size

    @pl.when(step == 0)
    def _():
        dmemory[...] = jnp.zeros_like(dmemory)
        nexts[...] = jnp.zeros_like(nexts)
        dtaps_out[...] = jnp.zeros_like(dtaps_out)
        dgain_out[...] = jnp.zeros_like(dgain_out)

    lanes = iota((size, HD), 1)
    for row in range(rows):
        masks = Masks(starts, row, base, size)
        place_next = base + size + iota((8, HD), 0)
        start_next = doc_start(starts, row, place_next)
        inside_next = [(place_next - i >= start_next).astype(F32) for i in range(KCONV)]
        rate_grads = jnp.zeros((size, HD), F32)
        for head in range(heads):
            pair = row * heads + head

            def group(kind):
                at = (kind * heads + head) * HD
                cur = lin[0, 0, row, 0, :, at : at + HD].astype(BF16).astype(F32)
                tail = edge[0, 0, row, 0, :, at : at + HD].astype(BF16).astype(F32)
                shifted, conv = conv_of(cur, tail, taps[:, at : at + HD], masks)
                sig = jax.nn.sigmoid(conv)
                return shifted, conv * sig, sig * (1.0 + conv * (1.0 - sig))

            def group_back(kind, shifted, slope, grad):
                at = (kind * heads + head) * HD
                dconv = grad * slope
                after = nexts[row, :, at : at + HD]
                total = None
                for i in range(KCONV):
                    dtaps_out[i : i + 1, at : at + HD] += jnp.sum(shifted[i] * dconv, axis=0, keepdims=True)
                    back = shift_up(dconv * masks.inside[i], after * inside_next[i], i) * taps[i : i + 1, at : at + HD]
                    total = back if total is None else total + back
                nexts[row, :, at : at + HD] = dconv[:8]
                dlin_out[0, 0, row, 0, :, at : at + HD] = total.astype(BF16)

            q_shift, query, q_slope = group(0)
            k_shift, key, k_slope = group(1)
            v_shift, _, v_slope = group(2)
            q_unit, k_unit = unit(query), unit(key)
            query = query * q_unit
            key = key * k_unit
            at = 3 * heads * HD + head
            rate = jnp.broadcast_to(
                jax.nn.sigmoid(lin[0, 0, row, 0, :, at : at + 1]), (size, HD)
            )
            rate_sq = rate if size == HD else rate[:, :size]

            at = head * HD
            mixed = mixed_in[0, 0, row, 0, :, at : at + HD]
            dhead = grad_in[0, 0, row, 0, :, at : at + HD].astype(F32)
            stat = lax.rsqrt(jnp.mean(mixed * mixed, axis=-1, keepdims=True) + EPS)
            scaled = mixed * stat
            dgain_out[:, at : at + HD] += jnp.sum(dhead * scaled, axis=0, keepdims=True)
            weighted = dhead * gain[:, at : at + HD]
            dmixed = stat * (weighted - scaled * jnp.mean(weighted * scaled, axis=-1, keepdims=True))

            fix, error, state = fix_in[0, pair], err_in[0, pair], mem_in[0, pair]
            dstate = dmemory[pair]
            gram = mm(key, jnp.concatenate([key, query], axis=0), 1, 1)
            gram_kk = gram[:, :size]
            attend_t = gram[:, size:] * masks.diag_t
            dfix = mm(attend_t, dmixed) + mm(key * masks.last_doc, dstate)
            dright = mm(inv_in[0, pair], dfix, 0, 0)
            both = mm(jnp.concatenate([dmixed, -dright], axis=0), fix, 1, 1)
            dattend = both[:size] * masks.diag
            dlower = both[size:] * masks.strict
            dlower_gram = dlower * rate_sq
            drate = jnp.sum(dright * error, axis=-1, keepdims=True) + jnp.sum(
                dlower * gram_kk, axis=-1, keepdims=True
            )
            dread_q = masks.carry_in * dmixed
            dread_k = -(rate * masks.carry_in * dright)
            dread = jnp.concatenate([dread_q, dread_k], axis=0)
            stacked = jnp.concatenate([query, key], axis=0)
            from_state = mm(dread, state, 1, 1)
            dquery = from_state[:size] + mm(dattend, key)
            dkey = (
                from_state[size:]
                + mm(dattend, query, 0, 0)
                + mm(dlower_gram + dlower_gram.T, key)
                + masks.last_doc * mm(fix, dstate, 1, 1)
            )
            dmemory[pair] = masks.carry_last * dstate + mm(stacked, dread, 0, 0)
            dvalue = rate * dright
            dquery = q_unit * (dquery - query * jnp.sum(dquery * query, axis=-1, keepdims=True))
            dkey = k_unit * (dkey - key * jnp.sum(dkey * key, axis=-1, keepdims=True))
            group_back(0, q_shift, q_slope, dquery)
            group_back(1, k_shift, k_slope, dkey)
            group_back(2, v_shift, v_slope, dvalue)
            rate_grads = jnp.where(lanes == head, drate * rate * (1.0 - rate), rate_grads)
        at = 3 * heads * HD
        dlin_out[0, 0, row, 0, :, at : at + HD] = rate_grads.astype(BF16)


def blocks_of(array, tokens):
    return array.reshape(tokens + array.shape[1:])


def chunk_at(step, place):
    block = (step // 2) ^ place[0]
    return block % 2, step % 2, block // 2


def delta_forward(lin, taps, gain, starts, place, heads, layout):
    cores, halves, rows, folds, size = layout
    steps = cores * halves * folds
    pairs = rows * heads
    wide = lin.shape[1]

    def at_chunk(step, starts, place):
        core, half, fold = chunk_at(step, place)
        return core, half, 0, fold, 0, 0

    def token_block(columns):
        return pl.BlockSpec((1, 1, rows, 1, size, columns), at_chunk)

    def saved(columns, tall):
        return pl.BlockSpec((1, pairs, tall, columns), lambda step, starts, place: (step, 0, 0, 0))

    def tokens(columns, kind):
        return jax.ShapeDtypeStruct(layout + (columns,), kind)

    total = cores * halves * rows * folds * size
    outs = pl.pallas_call(
        functools.partial(forward_kernel, heads, rows, size),
        grid_spec=pltpu.PrefetchScalarGridSpec(
            num_scalar_prefetch=2,
            grid=(steps,),
            in_specs=[
                token_block(wide),
                pl.BlockSpec(taps.shape, lambda step, starts, place: (0, 0)),
                pl.BlockSpec(gain.shape, lambda step, starts, place: (0, 0)),
            ],
            out_specs=[
                token_block(heads * HD),
                token_block(heads * HD),
                saved(size, size),
                saved(HD, size),
                saved(HD, size),
                saved(HD, HD),
            ],
            scratch_shapes=[
                pltpu.VMEM((pairs, HD, HD), F32),
                pltpu.VMEM((rows, 8, 3 * heads * HD), F32),
            ],
        ),
        out_shape=[
            tokens(heads * HD, BF16),
            tokens(heads * HD, F32),
            jax.ShapeDtypeStruct((steps, pairs, size, size), BF16),
            jax.ShapeDtypeStruct((steps, pairs, size, HD), F32),
            jax.ShapeDtypeStruct((steps, pairs, size, HD), F32),
            jax.ShapeDtypeStruct((steps, pairs, HD, HD), F32),
        ],
        compiler_params=pltpu.CompilerParams(
            dimension_semantics=("arbitrary",), vmem_limit_bytes=40 * 1024 * 1024
        ),
        cost_estimate=pl.CostEstimate(
            flops=total * HD * HD * heads * 60, bytes_accessed=total * wide * 8, transcendentals=total * heads * HD * 3
        ),
        name="delta_forward",
    )(starts, place, lin.reshape(layout + (wide,)), taps, gain)
    low, mixed = outs[:2]
    return low.reshape(total, heads * HD), mixed, tuple(outs[2:])


def delta_backward(lin, taps, gain, starts, place, mixed, dhead, saves, heads, layout):
    cores, halves, rows, folds, size = layout
    steps = cores * halves * folds
    pairs = rows * heads
    wide = lin.shape[1]
    total = cores * halves * rows * folds * size

    def at_chunk(step, starts, place):
        core, half, fold = chunk_at(steps - 1 - step, place)
        return core, half, 0, fold, 0, 0

    def at_edge(step, starts, place):
        core, half, fold = chunk_at(jnp.maximum(steps - 2 - step, 0), place)
        return core, half, 0, fold, size // 8 - 1, 0

    def token_block(columns):
        return pl.BlockSpec((1, 1, rows, 1, size, columns), at_chunk)

    def saved(columns, tall):
        return pl.BlockSpec((1, pairs, tall, columns), lambda step, starts, place: (steps - 1 - step, 0, 0, 0))

    whole = lambda step, starts, place: (0, 0)
    lin_blocks = lin.reshape(layout + (wide,))
    dlin, dtaps, dgain = pl.pallas_call(
        functools.partial(backward_kernel, heads, rows, size, steps),
        grid_spec=pltpu.PrefetchScalarGridSpec(
            num_scalar_prefetch=2,
            grid=(steps,),
            in_specs=[
                token_block(wide),
                pl.BlockSpec((1, 1, rows, 1, 8, wide), at_edge),
                pl.BlockSpec(taps.shape, whole),
                pl.BlockSpec(gain.shape, whole),
                token_block(heads * HD),
                token_block(heads * HD),
                saved(size, size),
                saved(HD, size),
                saved(HD, size),
                saved(HD, HD),
            ],
            out_specs=[
                token_block(wide),
                pl.BlockSpec(taps.shape, whole),
                pl.BlockSpec(gain.shape, whole),
            ],
            scratch_shapes=[
                pltpu.VMEM((pairs, HD, HD), F32),
                pltpu.VMEM((rows, 8, 3 * heads * HD), F32),
            ],
        ),
        out_shape=[
            jax.ShapeDtypeStruct(layout + (wide,), BF16),
            jax.ShapeDtypeStruct(taps.shape, F32),
            jax.ShapeDtypeStruct(gain.shape, F32),
        ],
        compiler_params=pltpu.CompilerParams(
            dimension_semantics=("arbitrary",), vmem_limit_bytes=40 * 1024 * 1024
        ),
        cost_estimate=pl.CostEstimate(
            flops=total * HD * HD * heads * 60, bytes_accessed=total * wide * 10, transcendentals=total * heads * HD * 3
        ),
        name="delta_backward",
    )(starts, place, lin_blocks, lin_blocks, taps, gain, mixed, dhead.reshape(layout + (heads * HD,)), *saves)
    return dlin.reshape(total, wide), dtaps, dgain


def partner(value, axis, bit):
    count = lax.axis_size(axis)
    return lax.ppermute(value, axis, [(i, i ^ bit) for i in range(count)])


def gather_z(piece):
    return [piece] + [partner(piece, "z", k) for k in range(1, lax.axis_size("z"))]


def permute_z(array):
    rows, wide = array.shape
    count = lax.axis_size("z")
    place = lax.axis_index("z")
    blocks = [array[:, k * (wide // count) : (k + 1) * (wide // count)] for k in range(count)]
    bit = 1
    while bit < count:
        odd = (place & bit) != 0
        blocks = [jnp.where(odd, blocks[k ^ bit], blocks[k]) for k in range(count)]
        bit *= 2
    return jnp.concatenate(blocks, axis=1)


def steps_of(half):
    folds = lax.axis_size("s") // 2
    along_y = []
    bit = 2
    while bit < 2 * folds:
        along_y.append(("s", bit))
        bit *= 2
    return [("x", 1)] + along_y if half == 0 else along_y + [("x", 1)]


def axis_of(step):
    axis, bit = step
    return 0 if axis == "x" else 1


def gather_group(own):
    tokens, wide = own.shape
    folds = lax.axis_size("s") // 2
    halves = []
    for half in range(2):
        part = own[half * (tokens // 2) : (half + 1) * (tokens // 2)].reshape(1, 1, tokens // 2, wide)
        for step in steps_of(half):
            part = jnp.concatenate([part, partner(part, *step)], axis=axis_of(step))
        halves.append(part)
    mine = jnp.stack(halves)
    return mine, partner(mine, "s", 1)


def scatter_group(mine, theirs):
    _, _, folds, size, wide = mine.shape
    arrived = partner(theirs.astype(BF16), "s", 1)
    total = mine.astype(F32) + arrived.astype(F32)
    halves = []
    for half in range(2):
        part = total[half]
        for step in reversed(steps_of(half)):
            dim = axis_of(step)
            count = part.shape[dim] // 2
            keep = lax.slice_in_dim(part, 0, count, axis=dim)
            send = lax.slice_in_dim(part, count, 2 * count, axis=dim)
            part = keep + partner(send.astype(BF16), *step).astype(F32)
        halves.append(part.reshape(size, wide))
    return jnp.concatenate(halves, axis=0)


def norm_back(grad_out, scaled, stat, gain):
    weighted = grad_out * gain
    gain_grad = jnp.sum(grad_out * scaled, axis=0)
    input_grad = stat * (weighted - scaled * jnp.mean(weighted * scaled, axis=-1, keepdims=True))
    return (input_grad, gain_grad)


def dot(left, right, dim_left=1, dim_right=0):
    return lax.dot_general(left, right, (((dim_left,), (dim_right,)), ((), ())), preferred_element_type=F32)


def after(value, *others):
    return lax.optimization_barrier((value,) + others)[0]


def body(
    hidden_in,
    doc_lengths,
    norm1_gain,
    w_qkv,
    conv_weight,
    w_beta,
    head_gain,
    w_out,
    norm2_gain,
    w_gate_up,
    w_down,
    cotangent,
):
    deep, pair, seq = lax.axis_size("z"), lax.axis_size("x"), lax.axis_size("s")
    place_z, place_x, place_s = lax.axis_index("z"), lax.axis_index("x"), lax.axis_index("s")
    team = pair * seq
    devices = deep * team
    place = place_x * seq + place_s
    tokens, wide = hidden_in.shape[1:]
    folds, size = seq // 2, tokens // 2
    layout = (2, 2, pair, folds, size)
    rows_each = w_qkv.shape[0]
    total_heads = w_beta.shape[1]
    heads = total_heads // team
    span = heads * HD
    block = wide // deep
    taps_each = conv_weight.shape[1]

    small = jnp.concatenate(
        [
            norm1_gain,
            norm2_gain,
            head_gain,
            conv_weight.reshape(-1),
            w_beta.reshape(-1),
        ]
    )
    length = small.shape[0]
    padded = -(-length // 128) * 128
    small = jnp.pad(small, (0, padded - length))
    small = lax.all_to_all(
        jnp.broadcast_to(small[None], (devices, padded)), ("z", "x", "s"), 0, 0, tiled=True
    )
    gain_one = small[:, :rows_each].reshape(1, wide).astype(F32)
    gain_two = small[:, rows_each : 2 * rows_each].reshape(1, wide).astype(F32)
    gain_head = lax.dynamic_slice_in_dim(
        small[:, 2 * rows_each : 3 * rows_each].reshape(1, wide), place * span, span, axis=1
    ).astype(F32)
    at = 3 * rows_each
    taps = small[:, at : at + KCONV * taps_each].reshape(devices, KCONV, taps_each)
    taps = taps.transpose(1, 0, 2).reshape(KCONV, 3, team, span)
    taps = lax.dynamic_index_in_dim(taps, place, 2, False).reshape(KCONV, 3 * span).astype(F32)
    at = at + KCONV * taps_each
    betas = small[:, at:length].reshape(deep, team * rows_each, total_heads)
    betas = lax.dynamic_slice_in_dim(betas, place * heads, heads, axis=2)
    betas = lax.dynamic_index_in_dim(betas, place_z, 0, False)

    cut = w_qkv.reshape(rows_each, 3, team, span).transpose(2, 0, 1, 3).reshape(team, rows_each, 3 * span)
    cut = lax.all_to_all(cut, ("x", "s"), 0, 0, tiled=True).reshape(team * rows_each, 3 * span)
    cut = jnp.concatenate([cut, jnp.pad(betas, ((0, 0), (0, HD - heads)))], axis=1)
    qkv_pieces = gather_z(cut)
    mat_qkv = jnp.concatenate(qkv_pieces, axis=0)
    out_from = [(i, (i % deep) * team + i // deep) for i in range(devices)]
    out_piece = lax.ppermute(w_out, ("z", "x", "s"), out_from)
    out_pieces = gather_z(out_piece)

    def absolute_z(pieces):
        bit = 1
        while bit < deep:
            odd = (place_z & bit) != 0
            pieces = [jnp.where(odd, pieces[k ^ bit], pieces[k]) for k in range(deep)]
            bit *= 2
        return jnp.concatenate(pieces, axis=0)

    mat_out = absolute_z(out_pieces)

    units = w_gate_up.shape[2] // pair
    second = place_x == 1

    def swap_x(array, axis):
        low_part = lax.slice_in_dim(array, 0, units, axis=axis)
        high_part = lax.slice_in_dim(array, units, 2 * units, axis=axis)
        mine = jnp.where(second, high_part, low_part)
        theirs = partner(jnp.where(second, low_part, high_part), "x", 1)
        return jnp.where(second, theirs, mine), jnp.where(second, mine, theirs)

    gu_piece = jnp.concatenate(swap_x(w_gate_up.transpose(1, 0, 2), 2), axis=1)
    down_piece = jnp.concatenate(swap_x(w_down, 0), axis=1)
    gu_piece, down_piece = lax.optimization_barrier((gu_piece, down_piece, mat_qkv))[:2]
    mat_gu = jnp.concatenate(gather_z(gu_piece), axis=1)
    mat_down = jnp.concatenate(gather_z(down_piece), axis=1)
    mat_gate, mat_up = mat_gu[0], mat_gu[1]

    starts = jnp.sum(
        jnp.where(
            jnp.arange(doc_lengths.shape[1])[None, :] < jnp.arange(doc_lengths.shape[1])[:, None],
            doc_lengths[0][None, :],
            0,
        ),
        axis=1,
    )[None]
    starts = jnp.concatenate([starts, partner(starts, "x", 1)], axis=0)
    place_seq = place_s.reshape(1).astype(jnp.int32)

    resid = hidden_in[0].astype(F32)
    stat_one = lax.rsqrt(jnp.mean(resid * resid, axis=-1, keepdims=True) + EPS)
    scaled_one = resid * stat_one
    normed_one = jnp.concatenate(
        gather_group(permute_z((scaled_one * gain_one).astype(BF16))), axis=0
    ).reshape(-1, wide)
    linear = dot(normed_one, mat_qkv)
    head_low, mixed, saves = delta_forward(linear, taps, gain_head, starts, place_seq, heads, layout)
    half_rows = head_low.shape[0] // 2
    part_shape = (2, pair, folds, size, wide)
    attn = scatter_group(
        dot(head_low[:half_rows], mat_out).reshape(part_shape),
        dot(head_low[half_rows:], mat_out).reshape(part_shape),
    )
    middle = resid + attn
    stat_two = lax.rsqrt(jnp.mean(middle * middle, axis=-1, keepdims=True) + EPS)
    scaled_two = middle * stat_two

    normed_two = jnp.concatenate(
        gather_group(permute_z((scaled_two * gain_two).astype(BF16))), axis=0
    ).reshape(-1, wide)
    cot_rows = cotangent[0]
    cot_all = jnp.concatenate(gather_group(permute_z(cot_rows)), axis=0).reshape(-1, wide)
    gate = dot(normed_two, mat_gate)
    upper = dot(normed_two, mat_up)
    sig_gate = jax.nn.sigmoid(gate)
    act_low = (gate * sig_gate * upper).astype(BF16)
    ffn_out = scatter_group(
        dot(act_low[:half_rows], mat_down).reshape(part_shape),
        dot(act_low[half_rows:], mat_down).reshape(part_shape),
    )
    result = (middle + permute_z(ffn_out)).astype(BF16)

    act_grad = dot(cot_all, mat_down, 1, 1)
    gate_grad = (act_grad * upper * sig_gate * (1.0 + gate * (1.0 - sig_gate))).astype(BF16)
    upper_grad = (act_grad * gate * sig_gate).astype(BF16)

    def into_group(rows):
        return (dot(gate_grad[rows], mat_gate, 1, 1) + dot(upper_grad[rows], mat_up, 1, 1)).reshape(part_shape)

    normed_two_grad = permute_z(
        scatter_group(into_group(slice(0, half_rows)), into_group(slice(half_rows, None)))
    )

    def sum_z(of_block):
        total = None
        for k in reversed(range(deep)):
            part = of_block(k)
            if k:
                part = partner(part.astype(BF16), "z", k).astype(F32)
            total = part if total is None else total + part
        return total

    def columns(array, k):
        return array[:, k * block : (k + 1) * block]

    gu_sum = sum_z(
        lambda k: jnp.stack(
            [dot(columns(normed_two, k), gate_grad, 0, 0), dot(columns(normed_two, k), upper_grad, 0, 0)]
        )
    )
    down_sum = sum_z(lambda k: dot(act_low, columns(cot_all, k), 0, 0))

    def back_x(array, axis, join):
        half = array.shape[axis] // 2
        low_part = lax.slice_in_dim(array, 0, half, axis=axis)
        high_part = lax.slice_in_dim(array, half, 2 * half, axis=axis)
        mine = jnp.where(second, high_part, low_part)
        theirs = partner(jnp.where(second, low_part, high_part).astype(BF16), "x", 1).astype(F32)
        return jnp.concatenate(
            [jnp.where(second, theirs, mine), jnp.where(second, mine, theirs)], axis=join
        )

    gu_weight_grad = back_x(gu_sum, 1, 2).transpose(1, 0, 2)
    down_weight_grad = back_x(down_sum, 1, 0)

    middle_part, gain_two_grad = norm_back(normed_two_grad, scaled_two, stat_two, gain_two)
    middle_grad = cot_rows.astype(F32) + middle_part

    attn_low = jnp.concatenate(gather_group(middle_grad.astype(BF16)), axis=0).reshape(-1, wide)
    head_grad = dot(attn_low, mat_out, 1, 1)
    lin_grad, taps_grad, gain_head_grad = delta_backward(
        linear, taps, gain_head, starts, place_seq, mixed, head_grad, saves, heads, layout
    )
    qkv_sum = sum_z(lambda k: dot(columns(normed_one, k), lin_grad, 0, 0))
    out_part = dot(head_low, attn_low, 0, 0).reshape(deep, span // deep, wide)
    out_sum = sum_z(lambda k: lax.dynamic_index_in_dim(out_part, place_z ^ k, 0, False))
    out_weight_grad = lax.ppermute(
        out_sum.astype(BF16), ("z", "x", "s"), [(b, a) for a, b in out_from]
    ).astype(F32)
    qkv_back = lax.all_to_all(
        qkv_sum.astype(BF16).reshape(team, rows_each, 3 * span + HD), ("x", "s"), 0, 0, tiled=True
    ).astype(F32)
    qkv_weight_grad = (
        qkv_back[:, :, : 3 * span]
        .reshape(team, rows_each, 3, span)
        .transpose(1, 2, 0, 3)
        .reshape(rows_each, 3 * wide)
    )
    beta_weight_grad = (
        qkv_back[:, :, 3 * span : 3 * span + heads].transpose(1, 0, 2).reshape(rows_each, total_heads)
    )
    normed_grad = permute_z(
        scatter_group(
            dot(lin_grad[:half_rows], mat_qkv, 1, 1).reshape(part_shape),
            dot(lin_grad[half_rows:], mat_qkv, 1, 1).reshape(part_shape),
        )
    )
    resid_part, gain_one_grad = norm_back(normed_grad, scaled_one, stat_one, gain_one)
    input_grad = middle_grad + resid_part

    head_full = lax.dynamic_update_slice(jnp.zeros((1, wide), F32), gain_head_grad, (0, place * span))
    taps_full = lax.dynamic_update_slice(
        jnp.zeros((KCONV, 3, team, span), F32),
        taps_grad.reshape(KCONV, 3, 1, span),
        (0, 0, place, 0),
    )
    taps_full = taps_full.reshape(KCONV, devices, taps_each).transpose(1, 0, 2).reshape(devices, KCONV * taps_each)
    small_grads = jnp.concatenate(
        [
            gain_one_grad.reshape(devices, rows_each),
            gain_two_grad.reshape(devices, rows_each),
            head_full.reshape(devices, rows_each),
            taps_full,
        ],
        axis=1,
    )
    length = small_grads.shape[1]
    small_grads = jnp.pad(small_grads, ((0, 0), (0, -length % 128)))
    small_grads = jnp.sum(
        lax.all_to_all(small_grads, ("z", "x", "s"), 0, 0, tiled=True), axis=0
    )
    return (
        result[None],
        input_grad[None],
        small_grads[:rows_each],
        qkv_weight_grad,
        small_grads[3 * rows_each : length].reshape(KCONV, taps_each),
        beta_weight_grad,
        small_grads[2 * rows_each : 3 * rows_each],
        out_weight_grad,
        small_grads[rows_each : 2 * rows_each],
        gu_weight_grad,
        down_weight_grad,
    )


def solution(mesh):
    outer, seq = mesh.shape["dp"], mesh.shape["seq"]
    grid = Mesh(mesh.devices.reshape(outer // 2, 2, seq), ("z", "x", "s"))
    every = ("z", "x", "s")
    rows = ("z", "x")
    in_specs = (
        P(rows, "s", None),
        P(rows, None),
        P(every),
        P(every, None),
        P(None, every),
        P(every, None),
        P(every),
        P(every, None),
        P(every),
        P(rows, None, "s"),
        P("s", rows),
        P(rows, "s", None),
    )
    out_specs = (
        P(rows, "s", None),
        P(rows, "s", None),
        P(every),
        P(every, None),
        P(None, every),
        P(every, None),
        P(every),
        P(every, None),
        P(every),
        P(rows, None, "s"),
        P("s", rows),
    )
    return jax.shard_map(body, mesh=grid, in_specs=in_specs, out_specs=out_specs, check_vma=False)
```

```python
import functools
import jax
import jax.numpy as jnp
from jax import lax
from jax.experimental import pallas as pl
from jax.experimental.pallas import tpu as pltpu
from jax.sharding import Mesh, PartitionSpec as P

KCONV = 4
HD = 128
EPS = 1e-05
UNIT_EPS = 1e-06
F32 = jnp.float32
BF16 = jnp.bfloat16


def mm(left, right, dim_left=1, dim_right=0):
    return lax.dot_general(
        left.astype(BF16),
        right.astype(BF16),
        (((dim_left,), (dim_right,)), ((), ())),
        preferred_element_type=F32,
    )


def split(value):
    high = value.astype(BF16)
    return high, (value - high.astype(F32)).astype(BF16)


def mm3(left, right):
    lh, ll = split(left)
    rh, rl = split(right)
    return mm(lh, rh) + (mm(lh, rl) + mm(ll, rh))


def iota(shape, dim):
    return lax.broadcasted_iota(jnp.int32, shape, dim)


def doc_start(starts, row, place):
    found = jnp.zeros_like(place)
    for j in range(starts.shape[1]):
        first = starts[row, j]
        found = jnp.maximum(found, jnp.where(first <= place, first, 0))
    return found


def scalar_start(starts, row, place):
    found = jnp.int32(0)
    for j in range(starts.shape[1]):
        first = starts[row, j]
        found = jnp.maximum(found, jnp.where(first <= place, first, 0))
    return found


def shift_down(cur, tail, by):
    if by == 0:
        return cur
    rolled = pltpu.roll(cur, by, 0)
    edge = pltpu.roll(tail, by, 0)
    top = jnp.where(iota(edge.shape, 0) < by, edge, rolled[:8])
    return jnp.concatenate([top, rolled[8:]], axis=0)


def shift_up(cur, head, by):
    if by == 0:
        return cur
    size = cur.shape[0]
    rolled = pltpu.roll(cur, size - by, 0)
    edge = pltpu.roll(head, 8 - by, 0)
    last = jnp.where(iota(edge.shape, 0) >= 8 - by, edge, rolled[size - 8 :])
    return jnp.concatenate([rolled[: size - 8], last], axis=0)


class Masks:
    def __init__(self, starts, row, base, size):
        place = base + iota((size, HD), 0)
        start = doc_start(starts, row, place)
        self.inside = [(place - i >= start).astype(F32) for i in range(KCONV)]
        self.carry_in = (start < base).astype(F32)
        last = scalar_start(starts, row, base + size - 1)
        self.last_doc = (start == last).astype(F32)
        self.carry_last = (last < base).astype(F32)
        rows, cols = iota((size, size), 0), iota((size, size), 1)
        start_row = doc_start(starts, row, base + rows)
        start_col = doc_start(starts, row, base + cols)
        same = start_row == start_col
        self.strict = (same & (rows > cols)).astype(F32)
        self.diag = (same & (rows >= cols)).astype(F32)
        self.diag_t = (same & (rows <= cols)).astype(F32)


def conv_of(cur, tail, taps, masks):
    shifted = [shift_down(cur, tail, i) * masks.inside[i] for i in range(KCONV)]
    total = shifted[0] * taps[0:1]
    for i in range(1, KCONV):
        total = total + shifted[i] * taps[i : i + 1]
    return shifted, total


def unit(values):
    return lax.rsqrt(jnp.sum(values * values, axis=-1, keepdims=True) + UNIT_EPS)


def inverse(lowers, size):
    rows, cols = iota((size, size), 0), iota((size, size), 1)
    eye = (rows == cols).astype(F32)
    near = (rows // 16) == (cols // 16)
    lows = [jnp.where(near, lower, 0.0) for lower in lowers]
    founds = [eye - low for low in lows]
    squares = [mm3(low, low) for low in lows]
    for level in range(3):
        if level:
            squares = [mm3(square, square) for square in squares]
        founds = [found + mm3(found, square) for found, square in zip(founds, squares)]
    width = 16
    while width < size:
        near = ((rows // (2 * width)) == (cols // (2 * width))) & ((rows // width) != (cols // width))
        crosses = [mm3(found, jnp.where(near, lower, 0.0)) for found, lower in zip(founds, lowers)]
        founds = [found - mm3(cross, found) for found, cross in zip(founds, crosses)]
        width *= 2
    return founds


def forward_kernel(heads, rows, size, starts, place, lin, taps, gain, low_out, mixed_out, inv_out, fix_out, err_out, mem_out, memory, tails):
    step = pl.program_id(0)
    base = step * size

    @pl.when(step == 0)
    def _():
        memory[...] = jnp.zeros_like(memory)
        tails[...] = jnp.zeros_like(tails)

    every_mask = [Masks(starts, row, base, size) for row in range(rows)]
    pairs = [(row, head) for row in range(rows) for head in range(heads)]

    def group(row, head, kind):
        at = (kind * heads + head) * HD
        cur = lin[0, 0, row, 0, :, at : at + HD].astype(BF16).astype(F32)
        tail = tails[row, :, at : at + HD]
        _, conv = conv_of(cur, tail, taps[:, at : at + HD], every_mask[row])
        tails[row, :, at : at + HD] = cur[size - 8 :]
        return conv * jax.nn.sigmoid(conv)

    def rate_of(row, head):
        at = 3 * heads * HD + head
        return jnp.broadcast_to(jax.nn.sigmoid(lin[0, 0, row, 0, :, at : at + 1]), (size, HD))

    queries = [group(row, head, 0) for row, head in pairs]
    keys = [group(row, head, 1) for row, head in pairs]
    queries = [query * unit(query) for query in queries]
    keys = [key * unit(key) for key in keys]
    rates = [rate_of(row, head) for row, head in pairs]
    grams = [mm(jnp.concatenate([query, key], axis=0), key, 1, 1) for query, key in zip(queries, keys)]
    lowers = [
        (rate if size == HD else rate[:, :size]) * gram[size:] * every_mask[row].strict
        for (row, _), rate, gram in zip(pairs, rates, grams)
    ]
    inverses = inverse(lowers, size)
    for pair, (row, head) in enumerate(pairs):
        inv_out[0, pair] = inverses[pair].astype(BF16)
        mem_out[0, pair] = memory[pair]
    values = [group(row, head, 2) for row, head in pairs]
    reads = [
        mm(jnp.concatenate([query, key], axis=0), memory[pair])
        for pair, (query, key) in enumerate(zip(queries, keys))
    ]
    errors = [
        value - every_mask[row].carry_in * read[size:] for (row, _), value, read in zip(pairs, values, reads)
    ]
    fixes = [mm(inv, rate * error) for inv, rate, error in zip(inverses, rates, errors)]
    mixes = [
        every_mask[row].carry_in * read[:size] + mm(gram[:size] * every_mask[row].diag, fix)
        for (row, _), read, gram, fix in zip(pairs, reads, grams, fixes)
    ]
    for pair, (row, head) in enumerate(pairs):
        masks = every_mask[row]
        memory[pair] = masks.carry_last * memory[pair] + mm(keys[pair] * masks.last_doc, fixes[pair], 0, 0)
        fix_out[0, pair] = fixes[pair]
        err_out[0, pair] = errors[pair]
        mixed = mixes[pair]
        stat = lax.rsqrt(jnp.mean(mixed * mixed, axis=-1, keepdims=True) + EPS)
        at = head * HD
        low_out[0, 0, row, 0, :, at : at + HD] = (mixed * stat * gain[:, at : at + HD]).astype(BF16)
        mixed_out[0, 0, row, 0, :, at : at + HD] = mixed


def backward_kernel(heads, rows, size, steps, starts, place, lin, edge, taps, gain, mixed_in, grad_in, inv_in, fix_in, err_in, mem_in, dlin_out, dtaps_out, dgain_out, dmemory, nexts):
    step = pl.program_id(0)
    chunk = steps - 1 - step
    base = chunk * size

    @pl.when(step == 0)
    def _():
        dmemory[...] = jnp.zeros_like(dmemory)
        nexts[...] = jnp.zeros_like(nexts)
        dtaps_out[...] = jnp.zeros_like(dtaps_out)
        dgain_out[...] = jnp.zeros_like(dgain_out)

    pairs = [(row, head) for row in range(rows) for head in range(heads)]
    each = range(len(pairs))
    every_mask = [Masks(starts, row, base, size) for row in range(rows)]
    masks = [every_mask[row] for row, _ in pairs]
    next_place = base + size + iota((8, HD), 0)
    next_starts = [doc_start(starts, row, next_place) for row in range(rows)]
    inside_next = [[(next_place - i >= start).astype(F32) for i in range(KCONV)] for start in next_starts]

    def group(row, head, kind):
        at = (kind * heads + head) * HD
        cur = lin[0, 0, row, 0, :, at : at + HD].astype(BF16).astype(F32)
        tail = edge[0, 0, row, 0, :, at : at + HD].astype(BF16).astype(F32)
        shifted, conv = conv_of(cur, tail, taps[:, at : at + HD], every_mask[row])
        sig = jax.nn.sigmoid(conv)
        return shifted, conv * sig, sig * (1.0 + conv * (1.0 - sig))

    def group_back(row, head, kind, grad):
        at = (kind * heads + head) * HD
        shifted, _, slope = group(row, head, kind)
        dconv = grad * slope
        after = nexts[row, :, at : at + HD]
        total = None
        for i in range(KCONV):
            dtaps_out[i : i + 1, at : at + HD] += jnp.sum(shifted[i] * dconv, axis=0, keepdims=True)
            back = (
                shift_up(dconv * every_mask[row].inside[i], after * inside_next[row][i], i)
                * taps[i : i + 1, at : at + HD]
            )
            total = back if total is None else total + back
        nexts[row, :, at : at + HD] = dconv[:8]
        dlin_out[0, 0, row, 0, :, at : at + HD] = total.astype(BF16)

    def head_back(row, head):
        at = head * HD
        mixed = mixed_in[0, 0, row, 0, :, at : at + HD]
        dhead = grad_in[0, 0, row, 0, :, at : at + HD].astype(F32)
        stat = lax.rsqrt(jnp.mean(mixed * mixed, axis=-1, keepdims=True) + EPS)
        scaled = mixed * stat
        dgain_out[:, at : at + HD] += jnp.sum(dhead * scaled, axis=0, keepdims=True)
        weighted = dhead * gain[:, at : at + HD]
        return stat * (weighted - scaled * jnp.mean(weighted * scaled, axis=-1, keepdims=True))

    def rate_of(row, head):
        at = 3 * heads * HD + head
        return jnp.broadcast_to(jax.nn.sigmoid(lin[0, 0, row, 0, :, at : at + 1]), (size, HD))

    queries = [group(row, head, 0)[1] for row, head in pairs]
    keys = [group(row, head, 1)[1] for row, head in pairs]
    q_units, k_units = [unit(query) for query in queries], [unit(key) for key in keys]
    queries = [query * u for query, u in zip(queries, q_units)]
    keys = [key * u for key, u in zip(keys, k_units)]
    rates = [rate_of(row, head) for row, head in pairs]
    dmixes = [head_back(row, head) for row, head in pairs]
    grams = [mm(key, jnp.concatenate([key, query], axis=0), 1, 1) for query, key in zip(queries, keys)]
    dfixes = [
        mm(grams[p][:, size:] * masks[p].diag_t, dmixes[p]) + mm(keys[p] * masks[p].last_doc, dmemory[p])
        for p in each
    ]
    drights = [mm(inv_in[0, p], dfixes[p], 0, 0) for p in each]
    boths = [mm(jnp.concatenate([dmixes[p], -drights[p]], axis=0), fix_in[0, p], 1, 1) for p in each]
    dattends = [boths[p][:size] * masks[p].diag for p in each]
    dlowers = [boths[p][size:] * masks[p].strict for p in each]
    drates = [
        jnp.sum(drights[p] * err_in[0, p], axis=-1, keepdims=True)
        + jnp.sum(dlowers[p] * grams[p][:, :size], axis=-1, keepdims=True)
        for p in each
    ]
    dreads = [
        jnp.concatenate([masks[p].carry_in * dmixes[p], -(rates[p] * masks[p].carry_in * drights[p])], axis=0)
        for p in each
    ]
    from_states = [mm(dreads[p], mem_in[0, p], 1, 1) for p in each]
    dlowers = [dlowers[p] * (rates[p] if size == HD else rates[p][:, :size]) for p in each]
    dqueries = [from_states[p][:size] + mm(dattends[p], keys[p]) for p in each]
    dkeys = [
        from_states[p][size:]
        + mm(dattends[p], queries[p], 0, 0)
        + mm(dlowers[p] + dlowers[p].T, keys[p])
        + masks[p].last_doc * mm(fix_in[0, p], dmemory[p], 1, 1)
        for p in each
    ]
    for p in each:
        dmemory[p] = masks[p].carry_last * dmemory[p] + mm(
            jnp.concatenate([queries[p], keys[p]], axis=0), dreads[p], 0, 0
        )
    lanes = iota((size, HD), 1)
    rate_grads = [jnp.zeros((size, HD), F32)] * rows
    for p, (row, head) in enumerate(pairs):
        dquery = q_units[p] * (dqueries[p] - queries[p] * jnp.sum(dqueries[p] * queries[p], axis=-1, keepdims=True))
        dkey = k_units[p] * (dkeys[p] - keys[p] * jnp.sum(dkeys[p] * keys[p], axis=-1, keepdims=True))
        group_back(row, head, 0, dquery)
        group_back(row, head, 1, dkey)
        group_back(row, head, 2, rates[p] * drights[p])
        rate_grads[row] = jnp.where(lanes == head, drates[p] * rates[p] * (1.0 - rates[p]), rate_grads[row])
    at = 3 * heads * HD
    for row in range(rows):
        dlin_out[0, 0, row, 0, :, at : at + HD] = rate_grads[row].astype(BF16)


def chunk_at(step, place):
    block = (step // 2) ^ place[0]
    return block % 2, step % 2, block // 2


def delta_forward(lin, taps, gain, starts, place, heads, layout):
    cores, halves, rows, folds, size = layout
    steps = cores * halves * folds
    pairs = rows * heads
    wide = lin.shape[1]

    def at_chunk(step, starts, place):
        core, half, fold = chunk_at(step, place)
        return core, half, 0, fold, 0, 0

    def token_block(columns):
        return pl.BlockSpec((1, 1, rows, 1, size, columns), at_chunk)

    def saved(columns, tall):
        return pl.BlockSpec((1, pairs, tall, columns), lambda step, starts, place: (step, 0, 0, 0))

    def tokens(columns, kind):
        return jax.ShapeDtypeStruct(layout + (columns,), kind)

    total = cores * halves * rows * folds * size
    outs = pl.pallas_call(
        functools.partial(forward_kernel, heads, rows, size),
        grid_spec=pltpu.PrefetchScalarGridSpec(
            num_scalar_prefetch=2,
            grid=(steps,),
            in_specs=[
                token_block(wide),
                pl.BlockSpec(taps.shape, lambda step, starts, place: (0, 0)),
                pl.BlockSpec(gain.shape, lambda step, starts, place: (0, 0)),
            ],
            out_specs=[
                token_block(heads * HD),
                token_block(heads * HD),
                saved(size, size),
                saved(HD, size),
                saved(HD, size),
                saved(HD, HD),
            ],
            scratch_shapes=[
                pltpu.VMEM((pairs, HD, HD), F32),
                pltpu.VMEM((rows, 8, 3 * heads * HD), F32),
            ],
        ),
        out_shape=[
            tokens(heads * HD, BF16),
            tokens(heads * HD, F32),
            jax.ShapeDtypeStruct((steps, pairs, size, size), BF16),
            jax.ShapeDtypeStruct((steps, pairs, size, HD), F32),
            jax.ShapeDtypeStruct((steps, pairs, size, HD), F32),
            jax.ShapeDtypeStruct((steps, pairs, HD, HD), F32),
        ],
        compiler_params=pltpu.CompilerParams(
            dimension_semantics=("arbitrary",), vmem_limit_bytes=40 * 1024 * 1024
        ),
        cost_estimate=pl.CostEstimate(
            flops=total * HD * HD * heads * 600, bytes_accessed=total * wide * 8, transcendentals=0
        ),
        name="delta_forward",
    )(starts, place, lin.reshape(layout + (wide,)), taps, gain)
    low, mixed = outs[:2]
    return low.reshape(total, heads * HD), mixed, tuple(outs[2:])


def delta_backward(lin, taps, gain, starts, place, mixed, dhead, saves, heads, layout):
    cores, halves, rows, folds, size = layout
    steps = cores * halves * folds
    pairs = rows * heads
    wide = lin.shape[1]
    total = cores * halves * rows * folds * size

    def at_chunk(step, starts, place):
        core, half, fold = chunk_at(steps - 1 - step, place)
        return core, half, 0, fold, 0, 0

    def at_edge(step, starts, place):
        core, half, fold = chunk_at(jnp.maximum(steps - 2 - step, 0), place)
        return core, half, 0, fold, size // 8 - 1, 0

    def token_block(columns):
        return pl.BlockSpec((1, 1, rows, 1, size, columns), at_chunk)

    def saved(columns, tall):
        return pl.BlockSpec((1, pairs, tall, columns), lambda step, starts, place: (steps - 1 - step, 0, 0, 0))

    whole = lambda step, starts, place: (0, 0)
    lin_blocks = lin.reshape(layout + (wide,))
    dlin, dtaps, dgain = pl.pallas_call(
        functools.partial(backward_kernel, heads, rows, size, steps),
        grid_spec=pltpu.PrefetchScalarGridSpec(
            num_scalar_prefetch=2,
            grid=(steps,),
            in_specs=[
                token_block(wide),
                pl.BlockSpec((1, 1, rows, 1, 8, wide), at_edge),
                pl.BlockSpec(taps.shape, whole),
                pl.BlockSpec(gain.shape, whole),
                token_block(heads * HD),
                token_block(heads * HD),
                saved(size, size),
                saved(HD, size),
                saved(HD, size),
                saved(HD, HD),
            ],
            out_specs=[
                token_block(wide),
                pl.BlockSpec(taps.shape, whole),
                pl.BlockSpec(gain.shape, whole),
            ],
            scratch_shapes=[
                pltpu.VMEM((pairs, HD, HD), F32),
                pltpu.VMEM((rows, 8, 3 * heads * HD), F32),
            ],
        ),
        out_shape=[
            jax.ShapeDtypeStruct(layout + (wide,), BF16),
            jax.ShapeDtypeStruct(taps.shape, F32),
            jax.ShapeDtypeStruct(gain.shape, F32),
        ],
        compiler_params=pltpu.CompilerParams(
            dimension_semantics=("arbitrary",), vmem_limit_bytes=40 * 1024 * 1024
        ),
        cost_estimate=pl.CostEstimate(
            flops=total * HD * HD * heads * 700, bytes_accessed=total * wide * 10, transcendentals=0
        ),
        name="delta_backward",
    )(starts, place, lin_blocks, lin_blocks, taps, gain, mixed, dhead.reshape(layout + (heads * HD,)), *saves)
    return dlin.reshape(total, wide), dtaps, dgain


def partner(value, axis, bit):
    count = lax.axis_size(axis)
    return lax.ppermute(value, axis, [(i, i ^ bit) for i in range(count)])


OUTER = [(1, 0), (2, 3)]
INNER = [(0, 1), (3, 2)]
MIDDLE = [(1, 2), (2, 1)]


class Flight:
    def __init__(self, steps):
        self.steps = steps
        self.parts = next(steps)
        self.result = None

    def advance(self):
        try:
            self.parts = self.steps.send(self.parts)
        except StopIteration as end:
            self.parts, self.result = None, end.value

    def join(self, value):
        if self.parts is None:
            return value
        value, self.parts = lax.optimization_barrier((value, self.parts))
        self.advance()
        return value

    def land(self, *others):
        for other in others:
            self.parts = other.join(self.parts)
        self.advance()
        return self.result


def joined(value, *flights):
    for flight in flights:
        value = flight.join(value)
    return value


def gather_z(piece):
    count = lax.axis_size("z")
    if count == 4:
        one, three = yield [partner(piece, "z", 1), lax.ppermute(piece, "z", MIDDLE)]
        two, far = yield [lax.ppermute(three, "z", OUTER), lax.ppermute(one, "z", MIDDLE)]
        (last,) = yield [lax.ppermute(far, "z", OUTER)]
        return [piece, one, two + far, three + last]
    pieces = yield [partner(piece, "z", k) for k in range(1, count)]
    return [piece] + pieces


def sum_z(blocks):
    count = lax.axis_size("z")
    if count == 4:
        own, one, two, three = blocks
        (far,) = yield [lax.ppermute(three.astype(BF16), "z", INNER)]
        near, far = yield [
            lax.ppermute(two.astype(BF16), "z", INNER),
            lax.ppermute((two.astype(F32) + far.astype(F32)).astype(BF16), "z", MIDDLE),
        ]
        one, three = yield [
            partner((one.astype(F32) + far.astype(F32)).astype(BF16), "z", 1),
            lax.ppermute((three.astype(F32) + near.astype(F32)).astype(BF16), "z", MIDDLE),
        ]
        return own.astype(F32) + one.astype(F32) + three.astype(F32)
    parts = yield [partner(blocks[k].astype(BF16), "z", k) for k in range(1, count)]
    total = blocks[0].astype(F32)
    for part in parts:
        total = total + part.astype(F32)
    return total


def swapped_z(blocks, place):
    bit = 1
    while bit < len(blocks):
        odd = (place & bit) != 0
        blocks = [jnp.where(odd, blocks[k ^ bit], blocks[k]) for k in range(len(blocks))]
        bit *= 2
    return blocks


def permute_z(array):
    count = lax.axis_size("z")
    size = array.shape[1] // count
    blocks = [array[:, k * size : (k + 1) * size] for k in range(count)]
    return jnp.concatenate(swapped_z(blocks, lax.axis_index("z")), axis=1)


def steps_of(half):
    folds = lax.axis_size("s") // 2
    along_y = []
    bit = 2
    while bit < 2 * folds:
        along_y.append(("s", bit))
        bit *= 2
    return [("x", 1)] + along_y if half == 0 else along_y + [("x", 1)]


def axis_of(step):
    axis, bit = step
    return 0 if axis == "x" else 1


def gather_group(own):
    tokens, wide = own.shape
    parts = [own[: tokens // 2].reshape(1, 1, tokens // 2, wide), own[tokens // 2 :].reshape(1, 1, tokens // 2, wide)]
    plans = [steps_of(0), steps_of(1)]
    for number in range(len(plans[0])):
        arrived = yield [partner(part, *plan[number]) for part, plan in zip(parts, plans)]
        parts = [
            jnp.concatenate([part, other], axis=axis_of(plan[number]))
            for part, other, plan in zip(parts, arrived, plans)
        ]
    mine = jnp.stack(parts)
    (theirs,) = yield [partner(mine, "s", 1)]
    return jnp.concatenate([mine, theirs], axis=0).reshape(-1, wide)


def scatter_group(mine, theirs):
    _, _, folds, size, wide = mine.shape
    (arrived,) = yield [partner(theirs.astype(BF16), "s", 1)]
    total = mine.astype(F32) + arrived.astype(F32)
    parts = [total[0], total[1]]
    plans = [steps_of(0)[::-1], steps_of(1)[::-1]]
    for number in range(len(plans[0])):
        sends, keeps = [], []
        for part, plan in zip(parts, plans):
            dim = axis_of(plan[number])
            count = part.shape[dim] // 2
            keeps.append(lax.slice_in_dim(part, 0, count, axis=dim))
            sends.append(lax.slice_in_dim(part, count, 2 * count, axis=dim))
        arrived = yield [partner(send.astype(BF16), *plan[number]) for send, plan in zip(sends, plans)]
        parts = [keep + other.astype(F32) for keep, other in zip(keeps, arrived)]
    return jnp.concatenate([part.reshape(size, wide) for part in parts], axis=0)


def ended(flight):
    while flight.parts is not None:
        flight.advance()
    return flight.result


def norm_back(grad_out, scaled, stat, gain):
    weighted = grad_out * gain
    gain_grad = jnp.sum(grad_out * scaled, axis=0)
    input_grad = stat * (weighted - scaled * jnp.mean(weighted * scaled, axis=-1, keepdims=True))
    return (input_grad, gain_grad)


def dot(left, right, dim_left=1, dim_right=0):
    return lax.dot_general(left, right, (((dim_left,), (dim_right,)), ((), ())), preferred_element_type=F32)


def after(value, *others):
    return lax.optimization_barrier((value,) + others)[0]


def body(
    hidden_in,
    doc_lengths,
    norm1_gain,
    w_qkv,
    conv_weight,
    w_beta,
    head_gain,
    w_out,
    norm2_gain,
    w_gate_up,
    w_down,
    cotangent,
):
    deep, pair, seq = lax.axis_size("z"), lax.axis_size("x"), lax.axis_size("s")
    place_z, place_x, place_s = lax.axis_index("z"), lax.axis_index("x"), lax.axis_index("s")
    team = pair * seq
    devices = deep * team
    place = place_x * seq + place_s
    tokens, wide = hidden_in.shape[1:]
    folds, size = seq // 2, tokens // 2
    layout = (2, 2, pair, folds, size)
    rows_each = w_qkv.shape[0]
    total_heads = w_beta.shape[1]
    heads = total_heads // team
    span = heads * HD
    block = wide // deep
    taps_each = conv_weight.shape[1]

    cut = w_qkv.reshape(rows_each, 3, team, span).transpose(2, 0, 1, 3).reshape(team, rows_each, 3 * span)
    cut = lax.all_to_all(cut, ("x", "s"), 0, 0, tiled=True).reshape(team * rows_each, 3 * span)

    small = jnp.concatenate(
        [
            norm1_gain,
            norm2_gain,
            head_gain,
            conv_weight.reshape(-1),
            w_beta.reshape(-1),
        ]
    )
    length = small.shape[0]
    padded = -(-length // 128) * 128
    small = jnp.pad(small, (0, padded - length))
    small = lax.all_to_all(
        jnp.broadcast_to(after(small, cut)[None], (devices, padded)), ("z", "x", "s"), 0, 0, tiled=True
    )
    out_from = [(i, (i % deep) * team + i // deep) for i in range(devices)]

    def gather_out(piece):
        (piece,) = yield [lax.ppermute(piece, ("z", "x", "s"), out_from)]
        return (yield from gather_z(piece))

    units = w_gate_up.shape[2] // pair
    second = place_x == 1

    def swap_x(array, axis):
        low_part = lax.slice_in_dim(array, 0, units, axis=axis)
        high_part = lax.slice_in_dim(array, units, 2 * units, axis=axis)
        mine = jnp.where(second, high_part, low_part)
        (theirs,) = yield [partner(jnp.where(second, low_part, high_part), "x", 1)]
        return jnp.concatenate([jnp.where(second, theirs, mine), jnp.where(second, mine, theirs)], axis=1)

    starts = jnp.sum(
        jnp.where(
            jnp.arange(doc_lengths.shape[1])[None, :] < jnp.arange(doc_lengths.shape[1])[:, None],
            doc_lengths[0][None, :],
            0,
        ),
        axis=1,
    )[None]
    starts = jnp.concatenate([starts, partner(starts, "x", 1)], axis=0)
    place_seq = place_s.reshape(1).astype(jnp.int32)

    hidden_flight = Flight(gather_group(permute_z(hidden_in[0])))
    hidden_flight.parts, cut = lax.optimization_barrier((hidden_flight.parts, cut))
    hidden_flight.advance()
    qkv_flight = Flight(gather_z(cut))
    gu_swap = Flight(swap_x(w_gate_up.transpose(1, 0, 2), 2))
    hidden_flight.parts, small = lax.optimization_barrier((hidden_flight.parts, small))
    hidden_flight.land(qkv_flight, gu_swap)
    gain_one = small[:, :rows_each].reshape(1, wide).astype(F32)
    gain_two = small[:, rows_each : 2 * rows_each].reshape(1, wide).astype(F32)
    gain_head = lax.dynamic_slice_in_dim(
        small[:, 2 * rows_each : 3 * rows_each].reshape(1, wide), place * span, span, axis=1
    ).astype(F32)
    at = 3 * rows_each
    taps = small[:, at : at + KCONV * taps_each].reshape(devices, KCONV, taps_each)
    taps = taps.transpose(1, 0, 2).reshape(KCONV, 3, team, span)
    taps = lax.dynamic_index_in_dim(taps, place, 2, False).reshape(KCONV, 3 * span).astype(F32)
    at = at + KCONV * taps_each
    betas = small[:, at:length].reshape(deep, team * rows_each, total_heads)
    betas = swapped_z(list(lax.dynamic_slice_in_dim(betas, place * heads, heads, axis=2)), place_z)
    betas = jnp.pad(jnp.concatenate(betas, axis=0), ((0, 0), (0, HD - heads)))

    down_swap = Flight(swap_x(w_down, 0))
    out_flight = Flight(gather_out(after(w_out, cut)))
    hidden_flight.land(qkv_flight, down_swap, out_flight)
    hidden_all = ended(hidden_flight).astype(F32)
    gain_one_z = permute_z(gain_one)
    stat_all = lax.rsqrt(jnp.mean(hidden_all * hidden_all, axis=-1, keepdims=True) + EPS)
    normed_one = joined((hidden_all * stat_all * gain_one_z).astype(BF16), qkv_flight, out_flight)
    mat_qkv = jnp.concatenate([jnp.concatenate(ended(qkv_flight), axis=0), betas], axis=1)
    normed_one, gu_piece, down_piece, cot_rows = lax.optimization_barrier(
        (normed_one, gu_swap.result, down_swap.result, cotangent[0])
    )
    gu_flight = Flight(gather_z(gu_piece))
    cot_flight = Flight(gather_group(permute_z(cot_rows)))
    linear = joined(dot(normed_one, mat_qkv), out_flight, cot_flight)
    head_low, mixed, saves = delta_forward(linear, taps, gain_head, starts, place_seq, heads, layout)
    head_low = joined(head_low, gu_flight, out_flight, cot_flight)
    mat_out = jnp.concatenate(swapped_z(ended(out_flight), place_z), axis=0)
    half_rows = head_low.shape[0] // 2
    part_shape = (2, pair, folds, size, wide)
    attn_flight = Flight(
        scatter_group(
            dot(head_low[:half_rows], mat_out).reshape(part_shape),
            dot(head_low[half_rows:], mat_out).reshape(part_shape),
        )
    )
    attn_flight.land(cot_flight)
    attn_flight.land(gu_flight)
    down_flight = Flight(gather_z(after(down_piece, attn_flight.parts)))
    while attn_flight.parts is not None:
        attn_flight.land()
    resid = hidden_in[0].astype(F32)
    middle = resid + attn_flight.result
    stat_two = lax.rsqrt(jnp.mean(middle * middle, axis=-1, keepdims=True) + EPS)
    scaled_two = middle * stat_two

    cot_all = ended(cot_flight)
    normed_flight = Flight(gather_group(permute_z((scaled_two * gain_two).astype(BF16))))
    normed_flight.land(gu_flight)
    while normed_flight.parts is not None:
        normed_flight.land(down_flight)
    normed_two = normed_flight.result
    mat_gu = jnp.concatenate(ended(gu_flight), axis=1)
    mat_gate, mat_up = mat_gu[0], mat_gu[1]
    gate = dot(normed_two, mat_gate)
    upper = down_flight.join(dot(normed_two, mat_up))
    mat_down = jnp.concatenate(ended(down_flight), axis=1)

    def columns(array, k):
        return array[:, k * block : (k + 1) * block]

    sig_gate = jax.nn.sigmoid(gate)
    act_low = (gate * sig_gate * upper).astype(BF16)
    act_grad = dot(cot_all, mat_down, 1, 1)
    gate_grad = (act_grad * upper * sig_gate * (1.0 + gate * (1.0 - sig_gate))).astype(BF16)
    upper_grad = (act_grad * gate * sig_gate).astype(BF16)

    def into_group(rows):
        return (dot(gate_grad[rows], mat_gate, 1, 1) + dot(upper_grad[rows], mat_up, 1, 1)).reshape(part_shape)

    grads_theirs = into_group(slice(half_rows, None)).astype(BF16)
    grads_mine = into_group(slice(0, half_rows))
    grad_flight = Flight(scatter_group(grads_mine, grads_theirs))
    act_low, cot_all, normed_two, grads_theirs = lax.optimization_barrier((act_low, cot_all, normed_two, grads_theirs))

    def down_block(k):
        return dot(act_low, columns(cot_all, k), 0, 0).astype(BF16)

    def gu_block(k):
        rows = columns(normed_two, k)
        return jnp.stack([dot(rows, gate_grad, 0, 0).astype(BF16), dot(rows, upper_grad, 0, 0).astype(BF16)])

    down_sum = Flight(sum_z([down_block(k) for k in range(deep)]))
    gu_sum = Flight(sum_z([gu_block(k) for k in range(deep)]))
    grad_flight.land()
    grad_flight.land(down_sum)
    grad_flight.land(gu_sum)
    normed_two_grad = permute_z(ended(grad_flight))
    ffn_flight = Flight(
        scatter_group(
            dot(act_low[:half_rows], mat_down).reshape(part_shape),
            dot(act_low[half_rows:], mat_down).reshape(part_shape),
        )
    )

    def back_x(array, axis, join):
        half = array.shape[axis] // 2
        low_part = lax.slice_in_dim(array, 0, half, axis=axis)
        high_part = lax.slice_in_dim(array, half, 2 * half, axis=axis)
        mine = jnp.where(second, high_part, low_part)
        (theirs,) = yield [partner(jnp.where(second, low_part, high_part).astype(BF16), "x", 1)]
        theirs = theirs.astype(F32)
        return jnp.concatenate(
            [jnp.where(second, theirs, mine), jnp.where(second, mine, theirs)], axis=join
        )

    middle_part, gain_two_grad = norm_back(normed_two_grad, scaled_two, stat_two, gain_two)
    middle_grad = cot_rows.astype(F32) + middle_part

    dattn_flight = Flight(gather_group(middle_grad.astype(BF16)))
    dattn_flight.land(down_sum)
    dattn_flight.land(gu_sum, ffn_flight)
    attn_low = ended(dattn_flight)
    head_grad = joined(dot(attn_low, mat_out, 1, 1), down_sum)
    out_part = dot(head_low, attn_low, 0, 0).astype(BF16).reshape(deep, span // deep, wide)
    out_sum = Flight(sum_z(swapped_z(list(out_part), place_z)))
    down_back = Flight(back_x(ended(down_sum), 1, 0))
    lin_grad, taps_grad, gain_head_grad = delta_backward(
        linear, taps, gain_head, starts, place_seq, mixed, head_grad, saves, heads, layout
    )
    lin_grad = joined(lin_grad, gu_sum, out_sum, ffn_flight, down_back)
    gu_back = Flight(back_x(ended(gu_sum), 1, 2))

    def qkv_block(k):
        return dot(columns(normed_one, k), lin_grad[:, : 3 * span], 0, 0).astype(BF16)

    qkv_blocks = [qkv_block(k) for k in range(deep)]
    qkv_sum = Flight(sum_z(qkv_blocks))
    lin_grad_next, _ = lax.optimization_barrier((lin_grad, qkv_blocks[-1]))
    grads_theirs = dot(lin_grad_next[half_rows:], mat_qkv, 1, 1).astype(BF16).reshape(part_shape)
    grads_mine = dot(lin_grad_next[:half_rows], mat_qkv, 1, 1).reshape(part_shape)
    grads_mine = joined(grads_mine, qkv_sum, out_sum)
    last_flight = Flight(scatter_group(grads_mine, grads_theirs))
    last_flight.land(gu_back)
    last_flight.land(qkv_sum, out_sum, ffn_flight)
    beta_part = dot(normed_one, lin_grad[:, 3 * span :], 0, 0)[:, :heads]
    normed_grad = permute_z(ended(last_flight))
    stat_one = lax.rsqrt(jnp.mean(resid * resid, axis=-1, keepdims=True) + EPS)
    resid_part, _ = norm_back(normed_grad, resid * stat_one, stat_one, gain_one)
    input_grad = middle_grad + resid_part
    result = (middle + permute_z(ended(ffn_flight))).astype(BF16)
    gu_weight_grad = ended(gu_back).transpose(1, 0, 2)
    down_weight_grad = ended(down_back)
    out_weight_grad = lax.ppermute(
        ended(out_sum).astype(BF16), ("z", "x", "s"), [(b, a) for a, b in out_from]
    ).astype(F32)
    qkv_back = lax.all_to_all(
        ended(qkv_sum).astype(BF16).reshape(team, rows_each, 3 * span), ("x", "s"), 0, 0, tiled=True
    ).astype(F32)
    qkv_weight_grad = (
        qkv_back.reshape(team, rows_each, 3, span).transpose(1, 2, 0, 3).reshape(rows_each, 3 * wide)
    )

    head_full = lax.dynamic_update_slice(jnp.zeros((1, wide), F32), gain_head_grad, (0, place * span))
    taps_full = lax.dynamic_update_slice(
        jnp.zeros((KCONV, 3, team, span), F32),
        taps_grad.reshape(KCONV, 3, 1, span),
        (0, 0, place, 0),
    )
    taps_full = taps_full.reshape(KCONV, devices, taps_each).transpose(1, 0, 2).reshape(devices, KCONV * taps_each)
    beta_part = jnp.concatenate(swapped_z(list(beta_part.reshape(deep, block, heads)), place_z), axis=0)
    beta_full = lax.dynamic_update_slice(jnp.zeros((wide, total_heads), F32), beta_part, (0, place * heads))
    small_grads = jnp.concatenate(
        [
            gain_two_grad.reshape(devices, rows_each),
            head_full.reshape(devices, rows_each),
            taps_full,
            beta_full.reshape(devices, rows_each * total_heads),
        ],
        axis=1,
    )
    length = small_grads.shape[1]
    small_grads = jnp.pad(small_grads, ((0, 0), (0, -length % 128)))
    small_grads = jnp.sum(
        lax.all_to_all(small_grads, ("z", "x", "s"), 0, 0, tiled=True), axis=0
    )
    at = 2 * rows_each + KCONV * taps_each
    beta_weight_grad = small_grads[at:length].reshape(rows_each, total_heads)
    gain_one_grad = (
        jnp.sum(w_qkv.astype(F32) * qkv_weight_grad, axis=1)
        + jnp.sum(w_beta.astype(F32) * beta_weight_grad, axis=1)
    ) / norm1_gain.astype(F32)
    return (
        result[None],
        input_grad[None],
        gain_one_grad,
        qkv_weight_grad,
        small_grads[2 * rows_each : at].reshape(KCONV, taps_each),
        beta_weight_grad,
        small_grads[rows_each : 2 * rows_each],
        out_weight_grad,
        small_grads[:rows_each],
        gu_weight_grad,
        down_weight_grad,
    )


def solution(mesh):
    outer, seq = mesh.shape["dp"], mesh.shape["seq"]
    grid = Mesh(mesh.devices.reshape(outer // 2, 2, seq), ("z", "x", "s"))
    every = ("z", "x", "s")
    rows = ("z", "x")
    in_specs = (
        P(rows, "s", None),
        P(rows, None),
        P(every),
        P(every, None),
        P(None, every),
        P(every, None),
        P(every),
        P(every, None),
        P(every),
        P(rows, None, "s"),
        P("s", rows),
        P(rows, "s", None),
    )
    out_specs = (
        P(rows, "s", None),
        P(rows, "s", None),
        P(every),
        P(every, None),
        P(None, every),
        P(every, None),
        P(every),
        P(every, None),
        P(every),
        P(rows, None, "s"),
        P("s", rows),
    )
    return jax.shard_map(body, mesh=grid, in_specs=in_specs, out_specs=out_specs, check_vma=False)
```
